32 devices in a mesh: shot: 2 (over y), space: 16 (over z, x, core).
Axes of the slice: x: 2, y: 2, z: 4, core: 2. Of those that a mesh axis runs over, the one named last changes fastest.
Arguments:
- wave_prev: float32 [2, 256, 128, 128], P('shot', 'space'), may hold values from -6 to 6
- wave_now: float32 [2, 256, 128, 128], P('shot', 'space'), may hold values from -6 to 6
- velocity: float32 [256, 128, 128], P('space'), may hold values from 0.05 to 0.2
- probe_panel: float32 [4, 256, 128, 128], P(None, 'space', 'shot'), may hold values from -6 to 6
- source_depth: int32 [2], P('shot'), may hold values from 0 to 255
- source_column: int32 [2], P('shot'), may hold values from 0 to 16383
- source_strength: float32 [2], P('shot'), may hold values from 2 to 6
- receiver_wells: int32 [2, 512], P('shot'), may hold values from 0 to 16383
Outputs:
- hessian_action: float32 [4, 256, 128, 128], P(None, 'space', 'shot')
The draws below stay inside these ranges and needn't reach their ends.
All inputs are finite; a program needn't handle non-finite values.
Results may differ from the reference program's by a relative error of at most 0.0003.
Values sent between devices are 32-bit elements; how exact they have to be, the bound alone decides.
A program may use at most 128 MiB of HBM per device.

```python
import jax
import jax.numpy as jnp
from jax import lax

NPROBE = 4
NX = 128
NY = 128
REC = 512
NZ = 256
SHOTS = 2


def touch_ends(array, own_key, least, largest):
    shape = array.shape
    place = [jax.random.randint(jax.random.fold_in(own_key, axis), (), 0, shape[axis]) for axis in range(len(shape))]
    array = array.at[tuple(place)].set(least)
    longest = shape.index(max(shape))
    place[longest] = (place[longest] + 1) % shape[longest]
    return array.at[tuple(place)].set(largest)


def levels(key, dims, cuts, least, top_value):
    loudness = 1.0
    for dim, blocks in cuts:
        heights = jax.random.uniform(jax.random.fold_in(jax.random.fold_in(key, 6), dim), (blocks,), jnp.float32, least / len(cuts), top_value / len(cuts))
        loudness = loudness * jnp.repeat(jnp.exp(heights), dims[dim] // blocks).reshape((-1,) + (1,) * (len(dims) - 1 - dim))
    return loudness


def gaussian(stream_key, shape, spread, limit, pieces=(), kind=jnp.bfloat16):
    array = jax.random.normal(stream_key, shape, jnp.float32) * spread
    if len(pieces) > 0:
        array = levels(stream_key, shape, pieces, -0.22, 0.18) * array
    return jnp.clip(array, min=-limit, max=limit).astype(kind)


def setup_inputs(seed: int = 0) -> dict:
    seeds = jax.random.split(jax.random.key(seed), 9)
    return {
        "wave_prev": gaussian(seeds[0], (SHOTS, NZ, NX, NY), 1.0, 6.0, ((0, 2), (1, 16)), jnp.float32),
        "wave_now": gaussian(seeds[1], (SHOTS, NZ, NX, NY), 1.0, 6.0, ((0, 2), (1, 16)), jnp.float32),
        "velocity": jnp.clip(0.05 + 0.15 * jax.random.uniform(seeds[2], (NZ, NX, NY), jnp.float32) ** levels(seeds[2], (NZ, NX, NY), ((0, 16),), -0.2, 0.2), 0.05, 0.2),
        "probe_panel": gaussian(seeds[3], (NPROBE, NZ, NX, NY), 1.0, 6.0, ((1, 16), (2, 2)), jnp.float32),
        "source_depth": jax.random.randint(seeds[4], (SHOTS,), 0, NZ).astype(jnp.int32),
        "source_column": jax.random.randint(seeds[5], (SHOTS,), 0, NX * NY).astype(jnp.int32),
        "source_strength": jnp.clip(2.0 + 4.0 * jax.random.uniform(seeds[6], (SHOTS,), jnp.float32) ** levels(seeds[6], (SHOTS,), ((0, 2),), -0.2, 0.2), 2.0, 6.0),
        "receiver_wells": touch_ends(jax.random.randint(seeds[7], (SHOTS, REC), 0, NX * NY), jax.random.fold_in(seeds[7], 1), 0, (NX * NY) - 1).astype(jnp.int32),
    }


CENTER = -205.0 / 72.0
WEIGHTS = (8.0 / 5.0, -1.0 / 5.0, 8.0 / 315.0, -1.0 / 560.0)


def laplace(padded):
    count_rows = padded.shape[-3] - 8
    middle = padded[..., 4:4 + count_rows, :, :]
    count_x = middle.shape[-2]
    count_y = middle.shape[-1]
    lead_pads = [(0, 0)] * (middle.ndim - 2)
    wide_x = jnp.pad(middle, lead_pads + [(4, 4), (0, 0)])
    wide_y = jnp.pad(middle, lead_pads + [(0, 0), (4, 4)])
    stencil = (3.0 * CENTER) * middle
    for offset in range(1, 5):
        weight = WEIGHTS[offset - 1]
        stencil = stencil + weight * (padded[..., 4 + offset:4 + offset + count_rows, :, :] + padded[..., 4 - offset:4 - offset + count_rows, :, :])
        stencil = stencil + weight * (wide_x[..., 4 + offset:4 + offset + count_x, :] + wide_x[..., 4 - offset:4 - offset + count_x, :])
        stencil = stencil + weight * (wide_y[..., 4 + offset:4 + offset + count_y] + wide_y[..., 4 - offset:4 - offset + count_y])
    return stencil


def zero_rim(field):
    return jnp.pad(field, [(0, 0)] * (field.ndim - 3) + [(4, 4), (0, 0), (0, 0)])


def reference(wave_prev, wave_now, velocity, probe_panel, source_depth, source_column, source_strength, receiver_wells):
    depth_ids = jnp.arange(NZ, dtype=jnp.int32)
    column_ids = jnp.arange(NX * NY, dtype=jnp.int32).reshape(NX, NY)

    def one_shot(carry, items):
        prev_field, now_field, depth, column, strength, wells = items
        born_zero = velocity * laplace(zero_rim(now_field))
        source_mark = ((depth_ids == depth)[:, None, None] & (column_ids == column)[None, :, :]).astype(jnp.float32)
        upcoming = 2.0 * now_field - prev_field + born_zero + source_mark * strength
        born_one = velocity * laplace(zero_rim(upcoming))
        first_field = probe_panel * born_zero
        second_field = 2.0 * first_field + velocity * laplace(zero_rim(first_field)) + probe_panel * born_one
        counts = jnp.zeros((NX * NY,), jnp.float32).at[wells].add(1.0).reshape(NX, NY)
        late_field = counts * second_field
        early_field = counts * first_field + 2.0 * late_field + laplace(zero_rim(velocity * late_field))
        return carry + (born_zero * early_field + born_one * late_field), None

    start = jnp.zeros((NPROBE, NZ, NX, NY), jnp.float32)
    summed, unused = lax.scan(one_shot, start, (wave_prev, wave_now, source_depth, source_column, source_strength, receiver_wells))
    return summed / SHOTS
```

```python
import functools

import jax
import jax.numpy as jnp
from jax import lax
from jax.experimental import pallas as pl
from jax.experimental.pallas import tpu as pltpu
from jax.sharding import PartitionSpec as P

CENTER = -205.0 / 72.0
WEIGHTS = (8.0 / 5.0, -1.0 / 5.0, 8.0 / 315.0, -1.0 / 560.0)
SCALED = (8064.0, -1008.0, 128.0, -9.0)
REACH = 4
EDGE = 8
MESH = pl.DeviceIdType.MESH


def kernel(
    shots,
    slabs,
    prev_ref,
    now_ref,
    vel_ref,
    probe_ref,
    depth_ref,
    column_ref,
    strength_ref,
    wells_ref,
    out_ref,
    now,
    prev,
    vel,
    velq,
    upc,
    bz,
    b1,
    bzq,
    b1q,
    cnt,
    cntq,
    pe,
    f,
    w,
    accz,
    accx,
    gotz,
    gotx,
    band,
    loc_sem,
    now_s,
    now_r,
    upc_s,
    upc_r,
    bzh_s,
    bzh_r,
    pz_s,
    pz_r,
    px_s,
    px_r,
    bzq_s,
    bzq_r,
    b1q_s,
    b1q_r,
    cnt_s,
    cnt_r,
    cz_s,
    cz_r,
    cx_s,
    cx_r,
):
    me = lax.axis_index("shot")
    slab = lax.axis_index("space")
    nz, nx, ny = vel_ref.shape
    probes, _, xw, _ = probe_ref.shape
    chunks = nz // REACH
    has_lo, has_hi = slab > 0, slab < slabs - 1
    has_left, has_right = me > 0, me < shots - 1
    lo, hi = jnp.maximum(slab - 1, 0), jnp.minimum(slab + 1, slabs - 1)
    left, right = jnp.maximum(me - 1, 0), jnp.minimum(me + 1, shots - 1)

    def remote(src, dst, ss, rs, dev):
        return pltpu.make_async_remote_copy(
            src_ref=src, dst_ref=dst, send_sem=ss, recv_sem=rs, device_id=dev, device_id_type=MESH
        )

    class Pair:
        def __init__(self, down, up, low, high):
            self.down, self.up, self.low, self.high = down, up, low, high

        def start(self):
            pl.when(self.low)(self.down.start)
            pl.when(self.high)(self.up.start)

        def wait_recv(self):
            pl.when(self.low)(self.up.wait_recv)
            pl.when(self.high)(self.down.wait_recv)

        def wait_send(self):
            pl.when(self.low)(self.down.wait_send)
            pl.when(self.high)(self.up.wait_send)

    def zpair(src_lo, src_hi, dst_lo, dst_hi, ss0, ss1, rs0, rs1):
        return Pair(
            remote(src_lo, dst_hi, ss0, rs1, (me, lo)),
            remote(src_hi, dst_lo, ss1, rs0, (me, hi)),
            has_lo,
            has_hi,
        )

    def xpair(src_lo, src_hi, dst_lo, dst_hi, ss0, ss1, rs0, rs1):
        return Pair(
            remote(src_lo, dst_hi, ss0, rs1, (left, slab)),
            remote(src_hi, dst_lo, ss1, rs0, (right, slab)),
            has_left,
            has_right,
        )

    barrier = pltpu.get_barrier_semaphore()

    def greet(dev):
        pl.semaphore_signal(barrier, inc=1, device_id=dev, device_id_type=MESH)

    pl.when(has_lo)(lambda: greet((me, lo)))
    pl.when(has_hi)(lambda: greet((me, hi)))
    for step in range(1, shots):
        greet((lax.rem(me + step, shots), slab))

    inner = pl.ds(EDGE, nx)
    mine = pl.ds(REACH, nz)
    top = pl.ds(0, REACH)
    bottom = pl.ds(REACH + nz, REACH)
    first_x = pl.multiple_of(me * xw, 8)
    rows = pl.ds(EDGE, xw)
    loads = [
        pltpu.make_async_copy(now_ref.at[0], now.at[mine, inner], loc_sem.at[0]),
        pltpu.make_async_copy(vel_ref, vel, loc_sem.at[1]),
        pltpu.make_async_copy(prev_ref.at[0], prev, loc_sem.at[2]),
        pltpu.make_async_copy(vel_ref.at[:, pl.ds(first_x, xw)], velq, loc_sem.at[3]),
        pltpu.make_async_copy(probe_ref, pe.at[:, mine, rows], loc_sem.at[4]),
    ]
    for load in loads:
        load.start()

    for ref in (now, upc, bz):
        ref[:, pl.ds(0, EDGE)] = jnp.zeros((nz + 2 * REACH, EDGE, ny), jnp.float32)
        ref[:, pl.ds(EDGE + nx, EDGE)] = jnp.zeros((nz + 2 * REACH, EDGE, ny), jnp.float32)

    def clear_end(place):
        for ref in (now, upc, bz):
            ref[place, inner] = jnp.zeros((REACH, nx, ny), jnp.float32)
        for p in range(probes):
            pe[p, place, rows] = jnp.zeros((REACH, xw, ny), jnp.float32)

    def clear_side(place):
        for p in range(probes):
            pe[p, mine, place] = jnp.zeros((nz, EDGE, ny), jnp.float32)

    pl.when(jnp.logical_not(has_lo))(lambda: clear_end(top))
    pl.when(jnp.logical_not(has_hi))(lambda: clear_end(bottom))
    pl.when(jnp.logical_not(has_left))(lambda: clear_side(pl.ds(0, EDGE)))
    pl.when(jnp.logical_not(has_right))(lambda: clear_side(pl.ds(EDGE + xw, EDGE)))
    w[pl.ds(0, REACH)] = jnp.zeros((REACH, xw + 4 * EDGE, ny), jnp.float32)
    w[pl.ds(REACH + nz, REACH)] = jnp.zeros((REACH, xw + 4 * EDGE, ny), jnp.float32)
    w[mine, pl.ds(0, 2 * EDGE)] = jnp.zeros((nz, 2 * EDGE, ny), jnp.float32)
    w[mine, pl.ds(2 * EDGE + xw, 2 * EDGE)] = jnp.zeros((nz, 2 * EDGE, ny), jnp.float32)

    arrivals = (
        shots - 1 + has_lo.astype(jnp.int32) + has_hi.astype(jnp.int32)
    )
    pl.semaphore_wait(barrier, arrivals)

    now_pair = zpair(
        now_ref.at[0, pl.ds(0, REACH)],
        now_ref.at[0, pl.ds(nz - REACH, REACH)],
        now.at[top, inner],
        now.at[bottom, inner],
        now_s.at[0], now_s.at[1], now_r.at[0], now_r.at[1],
    )
    now_pair.start()
    px_pair = xpair(
        probe_ref.at[:, :, pl.ds(0, EDGE)],
        probe_ref.at[:, :, pl.ds(xw - EDGE, EDGE)],
        pe.at[:, mine, pl.ds(0, EDGE)],
        pe.at[:, mine, pl.ds(EDGE + xw, EDGE)],
        px_s.at[0], px_s.at[1], px_r.at[0], px_r.at[1],
    )
    px_pair.start()
    pz_pair = zpair(
        probe_ref.at[:, pl.ds(0, REACH)],
        probe_ref.at[:, pl.ds(nz - REACH, REACH)],
        pe.at[:, top, rows],
        pe.at[:, bottom, rows],
        pz_s.at[0], pz_s.at[1], pz_r.at[0], pz_r.at[1],
    )
    pz_pair.start()

    row_id = lax.broadcasted_iota(jnp.int32, (ny, ny), 0)
    col_id = lax.broadcasted_iota(jnp.int32, (ny, ny), 1)
    apart = jnp.abs(row_id - col_id)
    half = jnp.zeros((ny, ny), jnp.float32)
    for k in range(1, REACH + 1):
        half = jnp.where(apart == k, SCALED[k - 1], half)
    half = half.astype(jnp.bfloat16)
    band[pl.ds(0, ny)] = half
    band[pl.ds(ny, ny)] = half

    wells = wells_ref[...]
    count = wells.shape[1]
    hot_x = (lax.broadcasted_iota(jnp.int32, (nx, count), 0) == lax.div(wells, ny)).astype(jnp.float32)
    hot_y = (lax.broadcasted_iota(jnp.int32, (ny, count), 0) == lax.rem(wells, ny)).astype(jnp.float32)
    cnt[...] = lax.dot_general(
        hot_x.astype(jnp.bfloat16),
        hot_y.astype(jnp.bfloat16),
        (((1,), (1,)), ((), ())),
        preferred_element_type=jnp.float32,
    )

    def partner_copy(step, kind):
        other = lax.rem(me + step, shots)
        source = lax.rem(me - step + shots, shots)
        start_x = pl.multiple_of(other * xw, 8)
        if kind == "cnt":
            return remote(cnt.at[pl.ds(start_x, xw)], cntq.at[me], cnt_s.at[other], cnt_r.at[me], (other, slab))
        if kind == "b1":
            return remote(
                b1.at[:, pl.ds(start_x, xw)], b1q.at[me], b1q_s.at[other], b1q_r.at[me], (other, slab)
            )
        place = {"bz": mine, "top": top, "bottom": bottom}[kind]
        index = {"bz": 0, "top": 1, "bottom": 2}[kind]
        return remote(
            bz.at[place, pl.ds(start_x, xw + 2 * EDGE)],
            bzq.at[me, place],
            bzq_s.at[other, index],
            bzq_r.at[me, index],
            (other, slab),
        )

    def send(kind):
        for step in range(1, shots):
            partner_copy(step, kind).start()

    send("cnt")
    cntq[me] = cnt[pl.ds(first_x, xw)]

    def laplace(ref, z, first, count):
        here = pl.ds(first, count)
        middle = ref[pl.ds(z, REACH), here]
        flat = middle.reshape(REACH * count, ny)
        high = flat.astype(jnp.bfloat16)
        low = (flat - high.astype(jnp.float32)).astype(jnp.bfloat16)
        along = jnp.dot(
            jnp.concatenate([high, low], axis=1), band[...], preferred_element_type=jnp.float32
        ).reshape(REACH, count, ny)
        total = (3.0 * CENTER) * middle + (1.0 / 5040.0) * along
        for k in range(1, REACH + 1):
            near = (
                ref[pl.ds(z + k, REACH), here]
                + ref[pl.ds(z - k, REACH), here]
                + ref[pl.ds(z, REACH), pl.ds(first + k, count)]
                + ref[pl.ds(z, REACH), pl.ds(first - k, count)]
            )
            total = total + WEIGHTS[k - 1] * near
        return total

    src_depth, src_column, src_strength = depth_ref[0], column_ref[0], strength_ref[0]
    xpart = min(64, nx)
    layer_id = lax.broadcasted_iota(jnp.int32, (REACH, xpart, ny), 0)
    cell_id = lax.broadcasted_iota(jnp.int32, (REACH, xpart, ny), 1) * ny + lax.broadcasted_iota(
        jnp.int32, (REACH, xpart, ny), 2
    )

    def step_zero(c):
        z = c * REACH
        for x0 in range(0, nx, xpart):
            xs = pl.ds(x0, xpart)
            xe = pl.ds(EDGE + x0, xpart)
            zs = pl.ds(z, REACH)
            ze = pl.ds(REACH + z, REACH)
            field = vel[zs, xs] * laplace(now, REACH + z, EDGE + x0, xpart)
            bz[ze, xe] = field
            hit = (layer_id + (slab * nz + z) == src_depth) & (cell_id + x0 * ny == src_column)
            upc[ze, xe] = (
                2.0 * now[ze, xe] - prev[zs, xs] + field + jnp.where(hit, src_strength, 0.0)
            )

    def step_one(c):
        z = c * REACH
        for x0 in range(0, nx, xpart):
            xs = pl.ds(x0, xpart)
            b1[pl.ds(z, REACH), xs] = vel[pl.ds(z, REACH), xs] * laplace(
                upc, REACH + z, EDGE + x0, xpart
            )

    def over(body, begin, end):
        def run(c, carry):
            body(c)
            return carry

        lax.fori_loop(begin, end, run, 0)

    loads[0].wait()
    loads[1].wait()
    loads[2].wait()
    over(step_zero, 1, chunks - 1)
    now_pair.wait_recv()

    def ends(body):
        over(lambda i: body(i * (chunks - 1)), 0, 2)

    ends(step_zero)

    def halo(ref, ss, rs):
        return zpair(
            ref.at[pl.ds(REACH, REACH), inner],
            ref.at[pl.ds(nz, REACH), inner],
            ref.at[top, inner],
            ref.at[bottom, inner],
            ss.at[0], ss.at[1], rs.at[0], rs.at[1],
        )

    upc_pair = halo(upc, upc_s, upc_r)
    upc_pair.start()
    bzh_pair = halo(bz, bzh_s, bzh_r)
    bzh_pair.start()
    send("bz")
    over(step_one, 1, chunks - 1)
    upc_pair.wait_recv()
    ends(step_one)
    send("b1")
    bzh_pair.wait_recv()
    send("top")
    send("bottom")
    own_bz = pltpu.make_async_copy(
        bz.at[:, pl.ds(first_x, xw + 2 * EDGE)], bzq.at[me], loc_sem.at[5]
    )
    own_b1 = pltpu.make_async_copy(b1.at[:, pl.ds(first_x, xw)], b1q.at[me], loc_sem.at[6])
    own_bz.start()
    own_b1.start()
    loads[3].wait()
    loads[4].wait()
    px_pair.wait_recv()
    pz_pair.wait_recv()
    own_bz.wait()
    own_b1.wait()

    def cz_pair(p):
        return zpair(
            accz.at[0, p], accz.at[1, p], gotz.at[0, p], gotz.at[1, p],
            cz_s.at[0, p], cz_s.at[1, p], cz_r.at[0, p], cz_r.at[1, p],
        )

    def cx_pair(p):
        return xpair(
            accx.at[0, p], accx.at[1, p], gotx.at[0, p], gotx.at[1, p],
            cx_s.at[0, p], cx_s.at[1, p], cx_r.at[0, p], cx_r.at[1, p],
        )

    wide = pl.ds(2 * EDGE, xw)

    def each_shot(t):
        shot = lax.rem(me + t, shots)

        @pl.when(t > 0)
        def _():
            start_x = pl.multiple_of(me * xw, 8)
            whole_x = pl.ds(start_x, xw + 2 * EDGE)
            for index, place in enumerate((mine, top, bottom)):
                remote(
                    bz.at[place, whole_x], bzq.at[shot, place],
                    bzq_s.at[shot, index], bzq_r.at[shot, index], (shot, slab),
                ).wait_recv()
            remote(
                b1.at[:, pl.ds(start_x, xw)], b1q.at[shot],
                b1q_s.at[shot], b1q_r.at[shot], (shot, slab),
            ).wait_recv()
            remote(
                cnt.at[pl.ds(start_x, xw)], cntq.at[shot], cnt_s.at[shot], cnt_r.at[shot], (shot, slab)
            ).wait_recv()

        def each_probe(p):
            @pl.when(t == 0)
            def _():
                out_ref[p] = jnp.zeros((nz, xw, ny), jnp.float32)
                for side in range(2):
                    accz[side, p] = jnp.zeros((REACH, xw, ny), jnp.float32)
                    accx[side, p] = jnp.zeros((nz, EDGE, ny), jnp.float32)

            f[top, rows] = pe[p, top, rows] * bzq[shot, top, rows]
            f[bottom, rows] = pe[p, bottom, rows] * bzq[shot, bottom, rows]

            def make_first(c):
                ze = pl.ds(REACH + c * REACH, REACH)
                f[ze] = pe[p, ze] * bzq[shot, ze]

            over(make_first, 0, chunks)

            def forward(c):
                z = c * REACH
                zs = pl.ds(z, REACH)
                ze = pl.ds(REACH + z, REACH)
                lap = laplace(f, REACH + z, EDGE, xw)
                first = f[ze, rows]
                v = velq[zs]
                one = b1q[shot, zs]
                tally = cntq[shot][None]
                second = 2.0 * first + v * lap + pe[p, ze, rows] * one
                late = tally * second
                w[ze, wide] = v * late
                out_ref[p, zs] += bzq[shot, ze, rows] * (tally * first + 2.0 * late) + one * late

            over(forward, 0, chunks)

            def adjoint(c):
                z = c * REACH
                zs = pl.ds(z, REACH)
                ze = pl.ds(REACH + z, REACH)
                out_ref[p, zs] += bzq[shot, ze, rows] * laplace(w, REACH + z, 2 * EDGE, xw)
                left_sum = jnp.zeros((REACH, EDGE, ny), jnp.float32)
                right_sum = jnp.zeros((REACH, EDGE, ny), jnp.float32)
                for k in range(1, REACH + 1):
                    left_sum += WEIGHTS[k - 1] * w[ze, pl.ds(EDGE + k, EDGE)]
                    right_sum += WEIGHTS[k - 1] * w[ze, pl.ds(2 * EDGE + xw - k, EDGE)]
                accx[0, p, zs] += bzq[shot, ze, pl.ds(0, EDGE)] * left_sum
                accx[1, p, zs] += bzq[shot, ze, pl.ds(EDGE + xw, EDGE)] * right_sum

            for j in range(1, REACH + 1):
                low_sum = jnp.zeros((xw, ny), jnp.float32)
                high_sum = jnp.zeros((xw, ny), jnp.float32)
                for k in range(j, REACH + 1):
                    low_sum += WEIGHTS[k - 1] * w[REACH + k - j, wide]
                    high_sum += WEIGHTS[k - 1] * w[REACH + nz - 1 - (k - j), wide]
                accz[0, p, REACH - j] += bzq[shot, REACH - j, rows] * low_sum
                accz[1, p, j - 1] += bzq[shot, REACH + nz + j - 1, rows] * high_sum
            pl.when(t == shots - 1)(lambda: cz_pair(p).start())
            over(adjoint, 0, chunks)
            pl.when(t == shots - 1)(lambda: cx_pair(p).start())

        over(each_probe, 0, probes)

    over(each_shot, 0, shots)

    scale = 1.0 / shots

    def finish(p):
        cz_pair(p).wait_recv()
        cx_pair(p).wait_recv()

        @pl.when(has_lo)
        def _():
            out_ref[p, pl.ds(0, REACH)] += gotz[0, p]

        @pl.when(has_hi)
        def _():
            out_ref[p, pl.ds(nz - REACH, REACH)] += gotz[1, p]

        @pl.when(has_left)
        def _():
            out_ref[p, :, pl.ds(0, EDGE)] += gotx[0, p]

        @pl.when(has_right)
        def _():
            out_ref[p, :, pl.ds(xw - EDGE, EDGE)] += gotx[1, p]

        out_ref[p] = out_ref[p] * scale
        cz_pair(p).wait_send()
        cx_pair(p).wait_send()

    over(finish, 0, probes)
    for pair in (now_pair, px_pair, pz_pair, upc_pair, bzh_pair):
        pair.wait_send()
    for kind in ("cnt", "bz", "b1", "top", "bottom"):
        for step in range(1, shots):
            partner_copy(step, kind).wait_send()


def per_device(shots, slabs, *arrays):
    nz, nx, ny = arrays[2].shape
    probes, _, xw, _ = arrays[3].shape
    tall = nz + 2 * REACH
    f32 = jnp.float32
    dma = pltpu.SemaphoreType.DMA
    two = [dma((2,))] * 2
    anywhere = pl.BlockSpec(memory_space=pl.ANY)
    scalar = pl.BlockSpec(memory_space=pltpu.SMEM)
    vector = pl.BlockSpec(memory_space=pltpu.VMEM)
    return pl.pallas_call(
        functools.partial(kernel, shots, slabs),
        out_shape=jax.ShapeDtypeStruct((probes, nz, xw, ny), f32),
        in_specs=[anywhere] * 4 + [scalar] * 3 + [vector],
        out_specs=vector,
        scratch_shapes=[
            pltpu.VMEM((tall, nx + 2 * EDGE, ny), f32),
            pltpu.VMEM((nz, nx, ny), f32),
            pltpu.VMEM((nz, nx, ny), f32),
            pltpu.VMEM((nz, xw, ny), f32),
            pltpu.VMEM((tall, nx + 2 * EDGE, ny), f32),
            pltpu.VMEM((tall, nx + 2 * EDGE, ny), f32),
            pltpu.VMEM((nz, nx, ny), f32),
            pltpu.VMEM((shots, tall, xw + 2 * EDGE, ny), f32),
            pltpu.VMEM((shots, nz, xw, ny), f32),
            pltpu.VMEM((nx, ny), f32),
            pltpu.VMEM((shots, xw, ny), f32),
            pltpu.VMEM((probes, tall, xw + 2 * EDGE, ny), f32),
            pltpu.VMEM((tall, xw + 2 * EDGE, ny), f32),
            pltpu.VMEM((tall, xw + 4 * EDGE, ny), f32),
            pltpu.VMEM((2, probes, REACH, xw, ny), f32),
            pltpu.VMEM((2, probes, nz, EDGE, ny), f32),
            pltpu.VMEM((2, probes, REACH, xw, ny), f32),
            pltpu.VMEM((2, probes, nz, EDGE, ny), f32),
            pltpu.VMEM((2 * ny, ny), jnp.bfloat16),
            dma((7,)),
            *two,
            *two,
            *two,
            *two,
            *two,
            dma((shots, 3)),
            dma((shots, 3)),
            dma((shots,)),
            dma((shots,)),
            dma((shots,)),
            dma((shots,)),
            dma((2, probes)),
            dma((2, probes)),
            dma((2, probes)),
            dma((2, probes)),
        ],
        compiler_params=pltpu.CompilerParams(
            collective_id=0, has_side_effects=True, vmem_limit_bytes=48 * 1024 * 1024
        ),
    )(*arrays)


def solution(mesh):
    return jax.shard_map(
        functools.partial(per_device, mesh.shape["shot"], mesh.shape["space"]),
        mesh=mesh,
        in_specs=(
            P("shot", "space", None, None),
            P("shot", "space", None, None),
            P("space", None, None),
            P(None, "space", "shot", None),
            P("shot"),
            P("shot"),
            P("shot"),
            P("shot", None),
        ),
        out_specs=P(None, "space", "shot", None),
        check_vma=False,
    )
```

```python
import functools

import jax
import jax.numpy as jnp
from jax import lax
from jax.experimental import pallas as pl
from jax.experimental.pallas import tpu as pltpu
from jax.sharding import PartitionSpec as P

CENTER = -205.0 / 72.0
WEIGHTS = (8.0 / 5.0, -1.0 / 5.0, 8.0 / 315.0, -1.0 / 560.0)
SCALED = (8064.0, -1008.0, 128.0, -9.0)
REACH = 4
EDGE = 8
MESH = pl.DeviceIdType.MESH


def kernel(
    shots,
    slabs,
    prev_ref,
    now_ref,
    vel_ref,
    probe_ref,
    depth_ref,
    column_ref,
    strength_ref,
    wells_ref,
    out_ref,
    now,
    prev,
    vel,
    velq,
    upc,
    bz,
    b1,
    bzq,
    b1q,
    cnt,
    cntq,
    pe,
    f,
    w,
    accz,
    accx,
    gotz,
    gotx,
    sendpx,
    gotpx,
    band,
    loc_sem,
    now_s,
    now_r,
    upc_s,
    upc_r,
    bzh_s,
    bzh_r,
    pz_s,
    pz_r,
    px_s,
    px_r,
    bzq_s,
    bzq_r,
    b1q_s,
    b1q_r,
    cnt_s,
    cnt_r,
    cz_s,
    cz_r,
    cx_s,
    cx_r,
):
    me = lax.axis_index("shot")
    slab = lax.axis_index("space")
    nz, nx, ny = vel_ref.shape
    probes, _, xw, _ = probe_ref.shape
    chunks = nz // REACH
    has_lo, has_hi = slab > 0, slab < slabs - 1
    has_left, has_right = me > 0, me < shots - 1
    lo, hi = jnp.maximum(slab - 1, 0), jnp.minimum(slab + 1, slabs - 1)
    left, right = jnp.maximum(me - 1, 0), jnp.minimum(me + 1, shots - 1)

    def remote(src, dst, ss, rs, dev):
        return pltpu.make_async_remote_copy(
            src_ref=src, dst_ref=dst, send_sem=ss, recv_sem=rs, device_id=dev, device_id_type=MESH
        )

    class Pair:
        def __init__(self, down, up, low, high):
            self.down, self.up, self.low, self.high = down, up, low, high

        def start(self):
            pl.when(self.low)(self.down.start)
            pl.when(self.high)(self.up.start)

        def wait_recv(self):
            pl.when(self.low)(self.up.wait_recv)
            pl.when(self.high)(self.down.wait_recv)

        def wait_send(self):
            pl.when(self.low)(self.down.wait_send)
            pl.when(self.high)(self.up.wait_send)

    def zpair(src_lo, src_hi, dst_lo, dst_hi, ss0, ss1, rs0, rs1):
        return Pair(
            remote(src_lo, dst_hi, ss0, rs1, (me, lo)),
            remote(src_hi, dst_lo, ss1, rs0, (me, hi)),
            has_lo,
            has_hi,
        )

    def xpair(src_lo, src_hi, dst_lo, dst_hi, ss0, ss1, rs0, rs1):
        return Pair(
            remote(src_lo, dst_hi, ss0, rs1, (left, slab)),
            remote(src_hi, dst_lo, ss1, rs0, (right, slab)),
            has_left,
            has_right,
        )

    barrier = pltpu.get_barrier_semaphore()

    def greet(dev):
        pl.semaphore_signal(barrier, inc=1, device_id=dev, device_id_type=MESH)

    pl.when(has_lo)(lambda: greet((me, lo)))
    pl.when(has_hi)(lambda: greet((me, hi)))
    for step in range(1, shots):
        greet((lax.rem(me + step, shots), slab))

    inner = pl.ds(EDGE, nx)
    mine = pl.ds(REACH, nz)
    top = pl.ds(0, REACH)
    bottom = pl.ds(REACH + nz, REACH)
    first_x = pl.multiple_of(me * xw, 8)
    rows = pl.ds(EDGE, xw)
    loads = [
        pltpu.make_async_copy(now_ref.at[0], now.at[mine, inner], loc_sem.at[0]),
        pltpu.make_async_copy(vel_ref, vel, loc_sem.at[1]),
        pltpu.make_async_copy(prev_ref.at[0], prev, loc_sem.at[2]),
        pltpu.make_async_copy(vel_ref.at[:, pl.ds(first_x, xw)], velq, loc_sem.at[3]),
        pltpu.make_async_copy(probe_ref, pe.at[:, mine, rows], loc_sem.at[4]),
    ]
    for load in loads:
        load.start()

    for ref in (now, upc, bz):
        ref[:, pl.ds(0, EDGE)] = jnp.zeros((nz + 2 * REACH, EDGE, ny), jnp.float32)
        ref[:, pl.ds(EDGE + nx, EDGE)] = jnp.zeros((nz + 2 * REACH, EDGE, ny), jnp.float32)

    def clear_end(place):
        for ref in (now, upc, bz):
            ref[place, inner] = jnp.zeros((REACH, nx, ny), jnp.float32)
        for p in range(probes):
            pe[p, place, rows] = jnp.zeros((REACH, xw, ny), jnp.float32)

    def clear_side(place):
        for p in range(probes):
            pe[p, mine, place] = jnp.zeros((nz, EDGE, ny), jnp.float32)
        for shot in range(shots):
            bzq[shot, mine, place] = jnp.zeros((nz, EDGE, ny), jnp.float32)

    pl.when(jnp.logical_not(has_lo))(lambda: clear_end(top))
    pl.when(jnp.logical_not(has_hi))(lambda: clear_end(bottom))
    pl.when(jnp.logical_not(has_left))(lambda: clear_side(pl.ds(0, EDGE)))
    pl.when(jnp.logical_not(has_right))(lambda: clear_side(pl.ds(EDGE + xw, EDGE)))
    w[pl.ds(0, REACH)] = jnp.zeros((REACH, xw + 4 * EDGE, ny), jnp.float32)
    w[pl.ds(REACH + nz, REACH)] = jnp.zeros((REACH, xw + 4 * EDGE, ny), jnp.float32)
    w[mine, pl.ds(0, 2 * EDGE)] = jnp.zeros((nz, 2 * EDGE, ny), jnp.float32)
    w[mine, pl.ds(2 * EDGE + xw, 2 * EDGE)] = jnp.zeros((nz, 2 * EDGE, ny), jnp.float32)

    arrivals = (
        shots - 1 + has_lo.astype(jnp.int32) + has_hi.astype(jnp.int32)
    )
    pl.semaphore_wait(barrier, arrivals)

    now_pair = zpair(
        now_ref.at[0, pl.ds(0, REACH)],
        now_ref.at[0, pl.ds(nz - REACH, REACH)],
        now.at[top, inner],
        now.at[bottom, inner],
        now_s.at[0], now_s.at[1], now_r.at[0], now_r.at[1],
    )
    now_pair.start()

    def pz_pair(p):
        return zpair(
            probe_ref.at[p, pl.ds(0, REACH)],
            probe_ref.at[p, pl.ds(nz - REACH, REACH)],
            pe.at[p, top, rows],
            pe.at[p, bottom, rows],
            pz_s.at[0, p], pz_s.at[1, p], pz_r.at[0, p], pz_r.at[1, p],
        )


    pair_z = nz // 2
    loads[4].wait()
    for p in range(probes):
        for part in range(2):
            zs = pl.ds(REACH + part * pair_z, pair_z)
            into = pl.ds(part * REACH, REACH)
            sendpx[0, p, :, into] = pe[p, zs, pl.ds(EDGE, REACH)]
            sendpx[1, p, :, into] = pe[p, zs, pl.ds(EDGE + xw - REACH, REACH)]
    px_pair = xpair(
        sendpx.at[0], sendpx.at[1], gotpx.at[0], gotpx.at[1],
        px_s.at[0], px_s.at[1], px_r.at[0], px_r.at[1],
    )
    px_pair.start()

    row_id = lax.broadcasted_iota(jnp.int32, (ny, ny), 0)
    col_id = lax.broadcasted_iota(jnp.int32, (ny, ny), 1)
    apart = jnp.abs(row_id - col_id)
    half = jnp.zeros((ny, ny), jnp.float32)
    for k in range(1, REACH + 1):
        half = jnp.where(apart == k, SCALED[k - 1], half)
    half = half.astype(jnp.bfloat16)
    band[pl.ds(0, ny)] = half
    band[pl.ds(ny, ny)] = half

    wells = wells_ref[...]
    count = wells.shape[1]
    hot_x = (lax.broadcasted_iota(jnp.int32, (nx, count), 0) == lax.div(wells, ny)).astype(jnp.float32)
    hot_y = (lax.broadcasted_iota(jnp.int32, (ny, count), 0) == lax.rem(wells, ny)).astype(jnp.float32)
    cnt[...] = lax.dot_general(
        hot_x.astype(jnp.bfloat16),
        hot_y.astype(jnp.bfloat16),
        (((1,), (1,)), ((), ())),
        preferred_element_type=jnp.float32,
    )

    ZERO = {
        "bz": (0, pl.ds(2 * REACH, nz - 2 * REACH)),
        "top": (1, top),
        "bottom": (2, bottom),
        "left": (3, mine),
        "right": (4, mine),
        "bz_low": (5, pl.ds(REACH, REACH)),
        "bz_high": (6, pl.ds(nz, REACH)),
    }
    ONE = {
        "b1": (0, pl.ds(REACH, nz - 2 * REACH)),
        "b1_low": (1, pl.ds(0, REACH)),
        "b1_high": (2, pl.ds(nz - REACH, REACH)),
    }

    def partner_copy(step, kind):
        other = lax.rem(me + step, shots)
        source = lax.rem(me - step + shots, shots)
        start_x = pl.multiple_of(other * xw, 8)
        if kind == "cnt":
            return remote(cnt.at[pl.ds(start_x, xw)], cntq.at[me], cnt_s.at[other], cnt_r.at[me], (other, slab))
        if kind in ONE:
            index, place = ONE[kind]
            return remote(
                b1.at[place, pl.ds(start_x, xw)],
                b1q.at[me, place],
                b1q_s.at[other, index],
                b1q_r.at[me, index],
                (other, slab),
            )
        index, place = ZERO[kind]
        if kind == "left":
            from_x, to_x = pl.ds(start_x, EDGE), pl.ds(0, EDGE)
        elif kind == "right":
            from_x, to_x = pl.ds(pl.multiple_of(start_x + EDGE + xw, 8), EDGE), pl.ds(EDGE + xw, EDGE)
        else:
            from_x, to_x = pl.ds(pl.multiple_of(start_x + EDGE, 8), xw), rows
        return remote(
            bz.at[place, from_x],
            bzq.at[me, place, to_x],
            bzq_s.at[other, index],
            bzq_r.at[me, index],
            (other, slab),
        )

    def needed(step, kind):
        other = lax.rem(me + step, shots)
        if kind == "left":
            return other > 0
        if kind == "right":
            return other < shots - 1
        return None

    def send(kind, wait=False):
        for step in range(1, shots):
            copy = partner_copy(step, kind)
            act = copy.wait_send if wait else copy.start
            need = needed(step, kind)
            if need is None:
                act()
            else:
                pl.when(need)(act)

    send("cnt")
    cntq[me] = cnt[pl.ds(first_x, xw)]

    def laplace(ref, z, first, count):
        here = pl.ds(first, count)
        middle = ref[pl.ds(z, REACH), here]
        flat = middle.reshape(REACH * count, ny)
        high = flat.astype(jnp.bfloat16)
        low = (flat - high.astype(jnp.float32)).astype(jnp.bfloat16)
        along = jnp.dot(
            jnp.concatenate([high, low], axis=1), band[...], preferred_element_type=jnp.float32
        ).reshape(REACH, count, ny)
        total = (3.0 * CENTER) * middle + (1.0 / 5040.0) * along
        for k in range(1, REACH + 1):
            near = (
                ref[pl.ds(z + k, REACH), here]
                + ref[pl.ds(z - k, REACH), here]
                + ref[pl.ds(z, REACH), pl.ds(first + k, count)]
                + ref[pl.ds(z, REACH), pl.ds(first - k, count)]
            )
            total = total + WEIGHTS[k - 1] * near
        return total

    src_depth, src_column, src_strength = depth_ref[0], column_ref[0], strength_ref[0]
    xpart = min(64, nx)
    layer_id = lax.broadcasted_iota(jnp.int32, (REACH, xpart, ny), 0)
    cell_id = lax.broadcasted_iota(jnp.int32, (REACH, xpart, ny), 1) * ny + lax.broadcasted_iota(
        jnp.int32, (REACH, xpart, ny), 2
    )

    def step_zero(c):
        z = c * REACH
        for x0 in range(0, nx, xpart):
            xs = pl.ds(x0, xpart)
            xe = pl.ds(EDGE + x0, xpart)
            zs = pl.ds(z, REACH)
            ze = pl.ds(REACH + z, REACH)
            field = vel[zs, xs] * laplace(now, REACH + z, EDGE + x0, xpart)
            bz[ze, xe] = field
            hit = (layer_id + (slab * nz + z) == src_depth) & (cell_id + x0 * ny == src_column)
            upc[ze, xe] = (
                2.0 * now[ze, xe] - prev[zs, xs] + field + jnp.where(hit, src_strength, 0.0)
            )

    def step_one(c):
        z = c * REACH
        for x0 in range(0, nx, xpart):
            xs = pl.ds(x0, xpart)
            b1[pl.ds(z, REACH), xs] = vel[pl.ds(z, REACH), xs] * laplace(
                upc, REACH + z, EDGE + x0, xpart
            )

    def over(body, begin, end):
        def run(c, carry):
            body(c)
            return carry

        lax.fori_loop(begin, end, run, 0)

    loads[0].wait()
    loads[1].wait()
    loads[2].wait()
    over(step_zero, 1, chunks - 1)
    send("bz")
    now_pair.wait_recv()

    def ends(body):
        over(lambda i: body(i * (chunks - 1)), 0, 2)

    ends(step_zero)

    def halo(ref, ss, rs):
        return zpair(
            ref.at[pl.ds(REACH, REACH), inner],
            ref.at[pl.ds(nz, REACH), inner],
            ref.at[top, inner],
            ref.at[bottom, inner],
            ss.at[0], ss.at[1], rs.at[0], rs.at[1],
        )

    upc_pair = halo(upc, upc_s, upc_r)
    upc_pair.start()
    bzh_pair = halo(bz, bzh_s, bzh_r)
    bzh_pair.start()
    send("bz_low")
    send("bz_high")
    send("left")
    send("right")

    def send_pz(p):
        pz_pair(p).start()

    over(send_pz, 0, probes)
    over(step_one, 1, chunks - 1)
    send("b1")
    upc_pair.wait_recv()
    ends(step_one)
    send("b1_low")
    send("b1_high")
    bzh_pair.wait_recv()
    send("top")
    send("bottom")
    own_bz = pltpu.make_async_copy(
        bz.at[:, pl.ds(first_x, xw + 2 * EDGE)], bzq.at[me], loc_sem.at[5]
    )
    own_b1 = pltpu.make_async_copy(b1.at[:, pl.ds(first_x, xw)], b1q.at[me], loc_sem.at[6])
    own_bz.start()
    own_b1.start()
    loads[3].wait()
    px_pair.wait_recv()

    @pl.when(has_left)
    def _():
        for p in range(probes):
            for part in range(2):
                zs = pl.ds(REACH + part * pair_z, pair_z)
                pe[p, zs, pl.ds(EDGE - REACH, REACH)] = gotpx[0, p, :, pl.ds(part * REACH, REACH)]

    @pl.when(has_right)
    def _():
        for p in range(probes):
            for part in range(2):
                zs = pl.ds(REACH + part * pair_z, pair_z)
                pe[p, zs, pl.ds(EDGE + xw, REACH)] = gotpx[1, p, :, pl.ds(part * REACH, REACH)]

    own_bz.wait()
    own_b1.wait()

    def cz_pair(p):
        return zpair(
            accz.at[0, p], accz.at[1, p], gotz.at[0, p], gotz.at[1, p],
            cz_s.at[0, p], cz_s.at[1, p], cz_r.at[0, p], cz_r.at[1, p],
        )

    def cx_pair(p):
        return xpair(
            accx.at[0, p], accx.at[1, p], gotx.at[0, p], gotx.at[1, p],
            cx_s.at[0, p], cx_s.at[1, p], cx_r.at[0, p], cx_r.at[1, p],
        )

    wide = pl.ds(2 * EDGE, xw)

    def each_shot(t):
        shot = lax.rem(me + t, shots)

        @pl.when(t > 0)
        def _():
            start_x = pl.multiple_of(me * xw, 8)

            def arrive(index, place, to_x):
                remote(
                    bz.at[place, to_x], bzq.at[shot, place, to_x],
                    bzq_s.at[shot, index], bzq_r.at[shot, index], (shot, slab),
                ).wait_recv()

            for kind in ("bz", "top", "bottom", "bz_low", "bz_high"):
                arrive(*ZERO[kind], rows)
            pl.when(has_left)(lambda: arrive(3, mine, pl.ds(0, EDGE)))
            pl.when(has_right)(lambda: arrive(4, mine, pl.ds(EDGE + xw, EDGE)))
            for index, place in ONE.values():
                remote(
                    b1.at[place, pl.ds(start_x, xw)], b1q.at[shot, place],
                    b1q_s.at[shot, index], b1q_r.at[shot, index], (shot, slab),
                ).wait_recv()
            remote(
                cnt.at[pl.ds(start_x, xw)], cntq.at[shot], cnt_s.at[shot], cnt_r.at[shot], (shot, slab)
            ).wait_recv()

        def each_probe(p):
            @pl.when(t == 0)
            def _():
                pz_pair(p).wait_recv()
                out_ref[p] = jnp.zeros((nz, xw, ny), jnp.float32)
                for side in range(2):
                    accz[side, p] = jnp.zeros((REACH, xw, ny), jnp.float32)
                    accx[side, p] = jnp.zeros((nz // 2, EDGE, ny), jnp.float32)

            f[top, rows] = pe[p, top, rows] * bzq[shot, top, rows]
            f[bottom, rows] = pe[p, bottom, rows] * bzq[shot, bottom, rows]

            def make_first(c):
                ze = pl.ds(REACH + c * REACH, REACH)
                f[ze] = pe[p, ze] * bzq[shot, ze]

            over(make_first, 0, chunks)

            def forward(c):
                z = c * REACH
                zs = pl.ds(z, REACH)
                ze = pl.ds(REACH + z, REACH)
                lap = laplace(f, REACH + z, EDGE, xw)
                first = f[ze, rows]
                v = velq[zs]
                one = b1q[shot, zs]
                tally = cntq[shot][None]
                second = 2.0 * first + v * lap + pe[p, ze, rows] * one
                late = tally * second
                w[ze, wide] = v * late
                out_ref[p, zs] += bzq[shot, ze, rows] * (tally * first + 2.0 * late) + one * late

            over(forward, 0, chunks)

            def adjoint(c):
                z = c * REACH
                zs = pl.ds(z, REACH)
                ze = pl.ds(REACH + z, REACH)
                out_ref[p, zs] += bzq[shot, ze, rows] * laplace(w, REACH + z, 2 * EDGE, xw)

            def sideways(c):
                for part in range(2):
                    ze = pl.ds(REACH + part * pair_z + c * REACH, REACH)
                    left_sum = jnp.zeros((REACH, REACH, ny), jnp.float32)
                    right_sum = jnp.zeros((REACH, REACH, ny), jnp.float32)
                    for k in range(1, REACH + 1):
                        left_sum += WEIGHTS[k - 1] * w[ze, pl.ds(EDGE + REACH + k, REACH)]
                        right_sum += WEIGHTS[k - 1] * w[ze, pl.ds(2 * EDGE + xw - k, REACH)]
                    place = (p, pl.ds(c * REACH, REACH), pl.ds(part * REACH, REACH))
                    accx[(0, *place)] += bzq[shot, ze, pl.ds(EDGE - REACH, REACH)] * left_sum
                    accx[(1, *place)] += bzq[shot, ze, pl.ds(EDGE + xw, REACH)] * right_sum

            for j in range(1, REACH + 1):
                low_sum = jnp.zeros((xw, ny), jnp.float32)
                high_sum = jnp.zeros((xw, ny), jnp.float32)
                for k in range(j, REACH + 1):
                    low_sum += WEIGHTS[k - 1] * w[REACH + k - j, wide]
                    high_sum += WEIGHTS[k - 1] * w[REACH + nz - 1 - (k - j), wide]
                accz[0, p, REACH - j] += bzq[shot, REACH - j, rows] * low_sum
                accz[1, p, j - 1] += bzq[shot, REACH + nz + j - 1, rows] * high_sum
            pl.when(t == shots - 1)(lambda: cz_pair(p).start())
            over(sideways, 0, chunks // 2)
            pl.when(t == shots - 1)(lambda: cx_pair(p).start())
            over(adjoint, 0, chunks)

        over(each_probe, 0, probes)

    over(each_shot, 0, shots)

    scale = 1.0 / shots

    def finish(p):
        cz_pair(p).wait_recv()
        cx_pair(p).wait_recv()

        @pl.when(has_lo)
        def _():
            out_ref[p, pl.ds(0, REACH)] += gotz[0, p]

        @pl.when(has_hi)
        def _():
            out_ref[p, pl.ds(nz - REACH, REACH)] += gotz[1, p]

        @pl.when(has_left)
        def _():
            for part in range(2):
                zs = pl.ds(part * pair_z, pair_z)
                out_ref[p, zs, pl.ds(0, REACH)] += gotx[0, p, :, pl.ds(part * REACH, REACH)]

        @pl.when(has_right)
        def _():
            for part in range(2):
                zs = pl.ds(part * pair_z, pair_z)
                out_ref[p, zs, pl.ds(xw - REACH, REACH)] += gotx[1, p, :, pl.ds(part * REACH, REACH)]

        out_ref[p] = out_ref[p] * scale
        cz_pair(p).wait_send()
        cx_pair(p).wait_send()

    over(finish, 0, probes)
    for pair in (now_pair, px_pair, upc_pair, bzh_pair):
        pair.wait_send()
    over(lambda p: pz_pair(p).wait_send(), 0, probes)
    for kind in ("cnt", *ZERO, *ONE):
        send(kind, wait=True)


def per_device(shots, slabs, *arrays):
    nz, nx, ny = arrays[2].shape
    probes, _, xw, _ = arrays[3].shape
    tall = nz + 2 * REACH
    f32 = jnp.float32
    dma = pltpu.SemaphoreType.DMA
    two = [dma((2,))] * 2
    anywhere = pl.BlockSpec(memory_space=pl.ANY)
    scalar = pl.BlockSpec(memory_space=pltpu.SMEM)
    vector = pl.BlockSpec(memory_space=pltpu.VMEM)
    return pl.pallas_call(
        functools.partial(kernel, shots, slabs),
        out_shape=jax.ShapeDtypeStruct((probes, nz, xw, ny), f32),
        in_specs=[anywhere] * 4 + [scalar] * 3 + [vector],
        out_specs=vector,
        scratch_shapes=[
            pltpu.VMEM((tall, nx + 2 * EDGE, ny), f32),
            pltpu.VMEM((nz, nx, ny), f32),
            pltpu.VMEM((nz, nx, ny), f32),
            pltpu.VMEM((nz, xw, ny), f32),
            pltpu.VMEM((tall, nx + 2 * EDGE, ny), f32),
            pltpu.VMEM((tall, nx + 2 * EDGE, ny), f32),
            pltpu.VMEM((nz, nx, ny), f32),
            pltpu.VMEM((shots, tall, xw + 2 * EDGE, ny), f32),
            pltpu.VMEM((shots, nz, xw, ny), f32),
            pltpu.VMEM((nx, ny), f32),
            pltpu.VMEM((shots, xw, ny), f32),
            pltpu.VMEM((probes, tall, xw + 2 * EDGE, ny), f32),
            pltpu.VMEM((tall, xw + 2 * EDGE, ny), f32),
            pltpu.VMEM((tall, xw + 4 * EDGE, ny), f32),
            pltpu.VMEM((2, probes, REACH, xw, ny), f32),
            pltpu.VMEM((2, probes, nz // 2, EDGE, ny), f32),
            pltpu.VMEM((2, probes, REACH, xw, ny), f32),
            pltpu.VMEM((2, probes, nz // 2, EDGE, ny), f32),
            pltpu.VMEM((2, probes, nz // 2, EDGE, ny), f32),
            pltpu.VMEM((2, probes, nz // 2, EDGE, ny), f32),
            pltpu.VMEM((2 * ny, ny), jnp.bfloat16),
            dma((7,)),
            *two,
            *two,
            *two,
            dma((2, probes)),
            dma((2, probes)),
            *two,
            dma((shots, 7)),
            dma((shots, 7)),
            dma((shots, 3)),
            dma((shots, 3)),
            dma((shots,)),
            dma((shots,)),
            dma((2, probes)),
            dma((2, probes)),
            dma((2, probes)),
            dma((2, probes)),
        ],
        compiler_params=pltpu.CompilerParams(
            collective_id=0, has_side_effects=True, vmem_limit_bytes=63 * 1024 * 1024
        ),
    )(*arrays)


def solution(mesh):
    return jax.shard_map(
        functools.partial(per_device, mesh.shape["shot"], mesh.shape["space"]),
        mesh=mesh,
        in_specs=(
            P("shot", "space", None, None),
            P("shot", "space", None, None),
            P("space", None, None),
            P(None, "space", "shot", None),
            P("shot"),
            P("shot"),
            P("shot"),
            P("shot", None),
        ),
        out_specs=P(None, "space", "shot", None),
        check_vma=False,
    )
```
